32 devices in a mesh: pts: 8 (over y, x, core), mem: 4 (over z).
Axes of the slice: x: 2, y: 2, z: 4, core: 2. Of those that a mesh axis runs over, the one named last changes fastest.
Arguments:
- ensemble: bfloat16 [64, 128, 4096], P('mem', None, 'pts'), may hold values from -4 to 4
- increment: float32 [128, 4096], P(None, 'pts'), may hold values from -8 to 8
- obs_weight: float32 [128, 4096], P(None, 'pts'), may hold values from 0.3 to 3
- vertical: bfloat16 [128, 128], replicated, may hold values from -0.5 to 0.5
- block_table: bfloat16 [12, 128, 128], replicated, may hold values from -0.15625 to 0.15625
- block_cols: int32 [32, 12], replicated, may hold values from 0 to 31, as said below
Outputs:
- weighted: float32 [128, 4096], P(None, 'pts')
- applied: float32 [128, 4096], P(None, 'pts')
The draws below stay inside these ranges and needn't reach their ends.
Inputs may be any that keep to these rules, and one draw needn't show every extreme that they name: `block_cols`: row r begins with r itself, and its 12 entries are different block indices.
All inputs are finite; a program needn't handle non-finite values.
Results may differ from the reference program's by a relative error of at most 0.012.
Values may be sent and summed in bfloat16 or wider, within the bound.
No kernel may reach another device: no remote copies, remote signals or barrier semaphores. Data moves between devices by JAX's collectives and lax.ppermute only.
A program may use at most 128 MiB of HBM per device.

```python
import math
import jax
import jax.numpy as jnp
from jax import lax

LV = 128
BLK = 128
NCOL = 12
P_SIZE = 4096
NB = 32
MEMBERS = 64


def draw_block_cols(key, part):
    row_keys = jax.random.split(jax.random.fold_in(key, 7), NB)
    orders = jax.vmap(lambda one_key: jax.random.permutation(one_key, NB - 1))(row_keys)[:, :NCOL - 1]
    row_ids = jnp.arange(NB, dtype=jnp.int32)[:, None]
    orders = orders.astype(jnp.int32)
    others = jnp.where(orders >= row_ids, orders + 1, orders)
    return jnp.concatenate([row_ids, others], axis=1).astype(jnp.int32)


def steps_of(stream_key, extent, cuts, low, high):
    factor_of, own = 1.0, jax.random.fold_in(stream_key, 6)
    for axis_at, parts in cuts:
        heights = jnp.exp(jax.random.uniform(jax.random.fold_in(own, axis_at), (parts,), jnp.float32, low / len(cuts), high / len(cuts)))
        factor_of = factor_of * jnp.repeat(heights, extent[axis_at] // parts).reshape([-1 if axis == axis_at else 1 for axis in range(len(extent))])
    return factor_of


def normal_values(key, dims, width, reach, cuts=(), kind=jnp.bfloat16):
    entries = jax.random.normal(key, dims, jnp.float32) * width
    if len(cuts) > 0:
        entries = steps_of(key, dims, cuts, -0.22, 0.18) * entries
    return jnp.clip(entries, min=-reach, max=reach).astype(kind)


def setup_inputs(seed: int = 0) -> dict:
    key_list = jax.random.split(jax.random.key(seed), 7)
    ensemble = normal_values(key_list[0], (MEMBERS, LV, P_SIZE), 0.3, 4.0, ((0, 4), (2, 8)))
    increment = normal_values(key_list[1], (LV, P_SIZE), 1.0, 8.0, ((1, 8),), jnp.float32)
    obs_weight = jnp.clip(jnp.exp(math.log(3.0) - 2.3025851 * jax.random.uniform(key_list[2], (LV, P_SIZE), jnp.float32) ** steps_of(key_list[2], (LV, P_SIZE), ((1, 8),), -0.2, 0.2)), 0.3, 3.0)
    vertical = normal_values(key_list[3], (LV, LV), LV ** -0.5, 0.5)
    block_table = normal_values(key_list[4], (NCOL, BLK, BLK), (NCOL * BLK) ** -0.5, 0.15625)
    block_cols = draw_block_cols(jax.random.fold_in(key_list[6], 71), 0)
    return dict(ensemble=ensemble, increment=increment, obs_weight=obs_weight, vertical=vertical, block_table=block_table, block_cols=block_cols)


def localize(values, block_table, block_cols):
    leading = values.shape[0]
    flattened = values.reshape(leading, NB, BLK)

    def add_slot(column, running):
        chosen = lax.dynamic_index_in_dim(block_cols, column, 1, keepdims=False)
        picked = jnp.take(flattened, chosen, axis=1).astype(jnp.float32)
        kernel = lax.dynamic_index_in_dim(block_table, column, 0, keepdims=False).astype(jnp.float32)
        return running + jnp.einsum("rnk,lk->rnl", picked, kernel)

    running = lax.fori_loop(0, NCOL, add_slot, jnp.zeros((leading, NB, BLK), jnp.float32))
    return running.reshape(leading, P_SIZE).astype(jnp.bfloat16)


def cov_apply(field_now, ensemble, vertical, block_table, block_cols):
    def member_step(summed, member):
        product = (member.astype(jnp.float32) * field_now).astype(jnp.bfloat16)
        vert_local = jnp.dot(vertical, product, preferred_element_type=jnp.float32).astype(jnp.bfloat16)
        horiz_local = lax.optimization_barrier(localize(vert_local, block_table, block_cols))
        return summed + member.astype(jnp.float32) * horiz_local.astype(jnp.float32), None

    summed, _ = lax.scan(member_step, jnp.zeros((LV, P_SIZE), jnp.float32), ensemble)
    return summed


def reference(ensemble, increment, obs_weight, vertical, block_table, block_cols):
    first_sum = cov_apply(increment, ensemble, vertical, block_table, block_cols)
    weighted = obs_weight * first_sum
    applied = cov_apply(weighted, ensemble, vertical, block_table, block_cols)
    return weighted, applied
```

```python
import functools

import jax
import jax.numpy as jnp
from jax import lax
from jax.experimental import pallas as pl
from jax.experimental.pallas import tpu as pltpu
from jax.sharding import PartitionSpec as P

BF = jnp.bfloat16
F32 = jnp.float32


def xor_permute(x, axis, size, k):
    return lax.ppermute(x, axis, [(i, i ^ k) for i in range(size)])


def cov_kernel(me_ref, cols_ref, ens_ref, fld_ref, vert_ref, tab_ref, own_ref, mate_ref, local_ref):
    shares, members, levels, width = ens_ref.shape
    slots = cols_ref.shape[1]
    blk = tab_ref.shape[1]
    per = width // blk
    me = me_ref[0]
    for d in range(shares):
        f = fld_ref[d].astype(F32)
        for m in range(members):
            product = (ens_ref[d ^ me, m].astype(F32) * f).astype(BF)
            mixed = jnp.dot(vert_ref[...], product, preferred_element_type=F32).astype(BF)
            for j in range(per):
                local_ref[d * per + j, m * levels:(m + 1) * levels, :] = mixed[:, j * blk:(j + 1) * blk]

    def chip(k, carry):
        rows = [
            jnp.concatenate([local_ref[cols_ref[k * 2 * per + q, s]] for s in range(slots)], axis=1)
            for q in range(2 * per)
        ]
        horiz = jnp.dot(jnp.concatenate(rows, axis=0), tab_ref[...], preferred_element_type=F32).astype(BF)
        for q in range(2 * per):
            core, j = q // per, q % per
            share = (2 * k + core) ^ me
            total = None
            for m in range(members):
                e = ens_ref[share, m, :, j * blk:(j + 1) * blk].astype(F32)
                row = (q * members + m) * levels
                term = e * horiz[row:row + levels].astype(F32)
                total = term if total is None else total + term
            (mate_ref if core else own_ref)[k, :, j * blk:(j + 1) * blk] = total.astype(BF)
        return carry

    lax.fori_loop(0, shares // 2, chip, 0)


def cov_call(me, cols, ens, fld, vertical, table):
    shares, members, levels, width = ens.shape
    blk = table.shape[1]
    half = jax.ShapeDtypeStruct((shares // 2, levels, width), BF)
    vmem = pl.BlockSpec(memory_space=pltpu.VMEM)
    smem = pl.BlockSpec(memory_space=pltpu.SMEM)
    return pl.pallas_call(
        cov_kernel,
        out_shape=(half, half),
        in_specs=[smem, smem, vmem, vmem, vmem, vmem],
        out_specs=(vmem, vmem),
        scratch_shapes=[pltpu.VMEM((shares * width // blk, members * levels, blk), BF)],
        compiler_params=pltpu.CompilerParams(vmem_limit_bytes=40 * 2**20),
    )(me, cols, ens, fld, vertical, table)


def per_device(ensemble, increment, obs_weight, vertical, block_table, block_cols):
    pts, mem = lax.axis_size("pts"), lax.axis_size("mem")
    members, levels, width = ensemble.shape
    slots, blk, _ = block_table.shape
    per = width // blk
    me = lax.axis_index("pts")

    ens = lax.all_to_all(
        ensemble.reshape(pts, members // pts, levels, width), "pts", split_axis=0, concat_axis=0, tiled=True
    )
    table = jnp.swapaxes(block_table, 1, 2).reshape(slots * blk, blk)
    relative = ((block_cols // per) ^ me) * per + block_cols % per
    cols = jnp.take(relative.reshape(pts, per, slots), jnp.arange(pts) ^ me, axis=0).reshape(pts * per, slots)

    def gather_field(x):
        same = [x] + [xor_permute(x, "pts", pts, 2 * k) for k in range(1, pts // 2)]
        same = jnp.stack(same)
        other = xor_permute(same, "pts", pts, 1)
        return jnp.stack([same, other], axis=1).reshape(pts, levels, width)

    def cov_sum(field):
        own, mate = cov_call(me.reshape(1), cols, ens, field, vertical, table)
        got = xor_permute(mate, "pts", pts, 1)
        chip = (own.astype(F32) + got.astype(F32)).astype(BF)
        total = chip[0].astype(F32)
        for k in range(1, pts // 2):
            total = total + xor_permute(chip[k], "pts", pts, 2 * k).astype(F32)
        plane = total.astype(BF)
        for k in range(1, mem):
            total = total + xor_permute(plane, "mem", mem, k).astype(F32)
        return total

    weighted = cov_sum(gather_field(increment.astype(BF))) * obs_weight
    applied = cov_sum(gather_field(weighted.astype(BF)))
    return weighted, applied


def solution(mesh):
    return jax.shard_map(
        per_device,
        mesh=mesh,
        in_specs=(P("mem", None, "pts"), P(None, "pts"), P(None, "pts"), P(), P(), P()),
        out_specs=(P(None, "pts"), P(None, "pts")),
        check_vma=False,
    )
```

```python
import functools

import jax
import jax.numpy as jnp
from jax import lax
from jax.experimental import pallas as pl
from jax.experimental.pallas import tpu as pltpu
from jax.sharding import PartitionSpec as P

BF = jnp.bfloat16
F32 = jnp.float32
VMEM = pl.BlockSpec(memory_space=pltpu.VMEM)
SMEM = pl.BlockSpec(memory_space=pltpu.SMEM)
PARAMS = pltpu.CompilerParams(vmem_limit_bytes=40 * 2**20)
COLUMNS = 4096
HOLD = 50 * 10**9


def xor_permute(x, axis, size, k):
    return lax.ppermute(x, axis, [(i, i ^ k) for i in range(size)])


def member_at(group, me, d, m):
    return group[d][m] if isinstance(group, list) else group[me ^ d, m]


def members_of(group):
    return (group[0].shape[0]) if isinstance(group, list) else group.shape[1]


def products(me, turn, groups, same_ref, other_ref, prod_ref):
    levels, width = same_ref.shape[1:]
    blk = prod_ref.shape[1]
    per = width // blk
    for d in range(2 * same_ref.shape[0]):
        f = (other_ref if d % 2 else same_ref)[(d // 2) ^ turn]
        at = 0
        for group in groups:
            for m in range(members_of(group)):
                product = (member_at(group, me, d, m) * f).T
                for j in range(per):
                    prod_ref[(me ^ d) * per + j, :, at:at + levels] = product[j * blk:(j + 1) * blk]
                at += levels


def local_sums(me, distances, cols_ref, groups, vert_ref, tab_ref, prod_ref, write):
    slots, blk, _ = tab_ref.shape
    columns = prod_ref.shape[2]
    levels = vert_ref.shape[0]
    nblk = prod_ref.shape[0]
    per = nblk // shares_of(groups[0])
    table = jnp.concatenate([tab_ref[s] for s in range(slots)], axis=1)
    batch = max(1, COLUMNS // (per * columns))
    for start in range(0, len(distances), batch):
        chosen = distances[start:start + batch]
        picked = []
        for d in chosen:
            for j in range(per):
                row = (me ^ d) * per + j
                picked.append(jnp.concatenate([prod_ref[cols_ref[s, row]] for s in range(slots)], axis=0))
        horiz = jnp.dot(table, jnp.concatenate(picked, axis=1), preferred_element_type=F32).astype(BF)
        for c, d in enumerate(chosen):
            total, at = None, 0
            for group in groups:
                for m in range(members_of(group)):
                    mixed = jnp.concatenate(
                        [horiz[:, (c * per + j) * columns + at:(c * per + j) * columns + at + levels] for j in range(per)],
                        axis=0,
                    )
                    local = lax.dot_general(
                        vert_ref[...], mixed, (((1,), (1,)), ((), ())), preferred_element_type=F32
                    )
                    term = member_at(group, me, d, m).astype(F32) * local
                    total = term if total is None else total + term
                    at += levels
            write(start + c, total)


def shares_of(group):
    return len(group) if isinstance(group, list) else group.shape[0]


def kernel(layout, with_products, out_distances, *refs):
    refs = list(refs)
    place_ref, cols_ref = refs.pop(0), refs.pop(0)
    me, turn = place_ref[0], place_ref[1]
    groups = []
    for count in layout:
        groups.append([refs.pop(0) for _ in range(count)] if count else refs.pop(0))
    vert_ref, tab_ref = refs.pop(0), refs.pop(0)
    if with_products:
        same_ref, other_ref = refs.pop(0), refs.pop(0)
    else:
        prod_ref = refs.pop(0)
    outs = [refs.pop(0) for _ in out_distances]
    if with_products:
        prod_ref = refs.pop(0)
        products(me, turn, groups, same_ref, other_ref, prod_ref)
    places = [(out_ref, i) for out_ref, distances in zip(outs, out_distances) for i in range(len(distances))]

    def write(i, total):
        out_ref, at = places[i]
        out_ref[at] = total.astype(out_ref.dtype)

    distances = [d for some in out_distances for d in some]
    local_sums(me, distances, cols_ref, groups, vert_ref, tab_ref, prod_ref, write)


def copy_kernel(x_ref, out_ref):
    out_ref[...] = x_ref[...]


def passed_on(x):
    return pl.pallas_call(
        copy_kernel, out_shape=jax.ShapeDtypeStruct(x.shape, x.dtype), in_specs=[VMEM], out_specs=VMEM,
        cost_estimate=pl.CostEstimate(flops=HOLD, bytes_accessed=0, transcendentals=0),
    )(x)


def per_device(ensemble, increment, obs_weight, vertical, block_table, block_cols):
    pts, mem = lax.axis_size("pts"), lax.axis_size("mem")
    members, levels, width = ensemble.shape
    slots, blk, _ = block_table.shape
    me = lax.axis_index("pts")
    plane = lax.axis_index("mem")
    cols = block_cols.T
    far = list(range(1, pts // 2))

    def call(groups, place, out_distances, dtype, prod=None, field=None):
        layout = [len(g) if isinstance(g, list) else 0 for g in groups]
        flat = [a for g in groups for a in (g if isinstance(g, list) else [g])]
        count = sum(g[0].shape[0] if isinstance(g, list) else g.shape[1] for g in groups)
        products_shape = jax.ShapeDtypeStruct((pts * width // blk, blk, count * levels), BF)
        args = [place, cols] + flat + [vertical, block_table] + (list(field) if field else [prod])
        outs = [jax.ShapeDtypeStruct((len(d), levels, width), dtype) for d in out_distances]
        return pl.pallas_call(
            functools.partial(kernel, layout, field is not None, out_distances),
            out_shape=outs + ([products_shape] if field else []),
            in_specs=[SMEM] * 2 + [VMEM] * (len(args) - 2),
            out_specs=[VMEM] * (len(outs) + bool(field)),
            compiler_params=PARAMS,
            cost_estimate=pl.CostEstimate(
                flops=8 * slots * blk * width * count * levels * sum(map(len, out_distances)), bytes_accessed=0,
                transcendentals=0,
            ),
        )(*args)

    def sum_over_mem(total):
        step = 1
        while step < mem:
            rounded = total.astype(BF)
            total = rounded.astype(F32) + xor_permute(rounded, "mem", mem, 2 * step - 1).astype(F32)
            step *= 2
        return total

    def cov_sum(groups, place, field):
        mate, prod = call(groups, place, [[2 * k + 1 for k in far] + [1]], BF, field=field)
        got = xor_permute(mate, "pts", pts, 1)
        (own,) = call(groups, place, [[2 * k for k in far]], BF, prod=prod)
        chip = (own.astype(F32) + got[:-1].astype(F32)).astype(BF)
        arrived = [xor_permute(chip[i], "pts", pts, 2 * k) for i, k in enumerate(far)]
        prod, _ = lax.optimization_barrier((prod, chip))
        (own,) = call(groups, place, [[0]], BF, prod=prod)
        total = own[0].astype(F32) + got[-1].astype(F32)
        for a in arrived:
            total = total + a.astype(F32)
        return sum_over_mem(total)

    rounded = increment.astype(BF)
    if pts // 2 == mem:
        pairs = [(p * mem + z, (p ^ (2 * z)) * mem + z) for p in range(pts) for z in range(mem)]
        fetched = passed_on(lax.ppermute(rounded, ("pts", "mem"), pairs))
        same = jnp.stack([fetched] + [xor_permute(fetched, "mem", mem, k) for k in range(1, mem)])
        place = jnp.stack([me, plane])
    else:
        same = jnp.stack([rounded] + [xor_permute(rounded, "pts", pts, 2 * k) for k in far])
        place = jnp.stack([me, jnp.zeros_like(me)])
    field = (same, xor_permute(same, "pts", pts, 1))

    split = ensemble.reshape(pts, members // pts, levels, width)
    groups = [lax.all_to_all(split, "pts", split_axis=0, concat_axis=0, tiled=True)]
    weighted = cov_sum(groups, place, field) * obs_weight

    rounded = weighted.astype(BF)
    same = jnp.stack([rounded] + [xor_permute(rounded, "pts", pts, 2 * k) for k in far])
    place = jnp.stack([me, jnp.zeros_like(me)])
    applied = cov_sum(groups, place, (same, xor_permute(same, "pts", pts, 1)))
    return weighted, applied


def solution(mesh):
    return jax.shard_map(
        per_device,
        mesh=mesh,
        in_specs=(P("mem", None, "pts"), P(None, "pts"), P(None, "pts"), P(), P(), P()),
        out_specs=(P(None, "pts"), P(None, "pts")),
        check_vma=False,
    )
```

```python
import functools

import jax
import jax.numpy as jnp
from jax import lax
from jax.experimental import pallas as pl
from jax.experimental.pallas import tpu as pltpu
from jax.sharding import PartitionSpec as P

BF = jnp.bfloat16
F32 = jnp.float32
VMEM = pl.BlockSpec(memory_space=pltpu.VMEM)
ANY = pl.BlockSpec(memory_space=pl.ANY)
PARAMS = pltpu.CompilerParams(vmem_limit_bytes=24 * 2**20)
COLUMNS = 4096
HOLD = 50 * 10**9


def products(me, turn, core, ens_ref, field_ref, prod_ref):
    _, members, levels, width = ens_ref.shape
    blk = prod_ref.shape[1]
    per = width // blk
    for k in range(field_ref.shape[0]):
        share = me ^ (2 * k + core)
        f = field_ref[k ^ turn]
        for m in range(members):
            product = (ens_ref[share, m] * f).T
            for j in range(per):
                prod_ref[share * per + j, :, m * levels:(m + 1) * levels] = product[j * blk:(j + 1) * blk]


def local_sums(shares, cols_ref, ens_ref, mat_ref, prod_ref, out_ref):
    _, members, levels, width = ens_ref.shape
    slots, blk = cols_ref.shape[0], prod_ref.shape[1]
    per = width // blk
    table = jnp.concatenate([mat_ref[s * blk:(s + 1) * blk, :blk] for s in range(slots)], axis=1)
    vertical = mat_ref[slots * blk:, :levels]
    batch = max(1, COLUMNS // (per * members * levels))
    for start in range(0, len(shares), batch):
        chosen = shares[start:start + batch]
        picked = []
        for share in chosen:
            for j in range(per):
                row = share * per + j
                picked.append(jnp.concatenate([prod_ref[cols_ref[s, row]] for s in range(slots)], axis=0))
        horiz = jnp.dot(table, jnp.concatenate(picked, axis=1), preferred_element_type=F32).astype(BF)
        for c, share in enumerate(chosen):
            total = None
            for m in range(members):
                parts = []
                for j in range(per):
                    at = ((c * per + j) * members + m) * levels
                    parts.append(horiz[:, at:at + levels])
                local = lax.dot_general(
                    vertical, jnp.concatenate(parts, axis=0), (((1,), (1,)), ((), ())),
                    preferred_element_type=F32,
                )
                term = ens_ref[share, m].astype(F32) * local
                total = term if total is None else total + term
            out_ref[start + c] = total.astype(BF)


def sums_kernel(cores, turned, wanted, *refs):
    refs = list(refs)
    cols_ref, copied = refs[-2:]
    copy = pltpu.make_async_copy(refs.pop(0), cols_ref, copied)
    copy.start()
    me = lax.axis_index("pts")
    ens_ref, mat_ref = refs.pop(0), refs.pop(0)
    field_refs = [refs.pop(0) for _ in cores]
    prod_ref = refs.pop(0) if len(cores) < 2 else None
    outs = [refs.pop(0) for _ in wanted]
    if cores:
        prod_ref = refs.pop(0)
        turn = lax.axis_index("mem") if turned else 0
        for core, field_ref in zip(cores, field_refs):
            products(me, turn, core, ens_ref, field_ref, prod_ref)
    copy.wait()
    for out_ref, (core, chips) in zip(outs, wanted):
        shares = [me ^ (2 * k + core) for k in chips]
        local_sums(shares, cols_ref, ens_ref, mat_ref, prod_ref, out_ref)


def products_kernel(ens_ref, field_ref, prod_ref):
    products(lax.axis_index("pts"), 0, 0, ens_ref, field_ref, prod_ref)


def copy_kernel(x_ref, out_ref):
    out_ref[...] = x_ref[...]


def passed_on(x):
    return pl.pallas_call(
        copy_kernel, out_shape=jax.ShapeDtypeStruct(x.shape, x.dtype), in_specs=[VMEM], out_specs=VMEM,
        compiler_params=PARAMS, cost_estimate=pl.CostEstimate(flops=HOLD, bytes_accessed=0, transcendentals=0),
    )(x)


def per_device(ensemble, increment, obs_weight, vertical, block_table, block_cols):
    pts, mem = lax.axis_size("pts"), lax.axis_size("mem")
    chips = pts // 2
    members, levels, width = ensemble.shape
    slots, blk, _ = block_table.shape
    share = members // pts
    cols = block_cols.T
    far = list(range(1, chips))
    wide = max(blk, levels)
    matrices = jnp.concatenate([
        jnp.pad(block_table.reshape(slots * blk, blk), ((0, 0), (0, wide - blk))),
        jnp.pad(vertical, ((0, 0), (0, wide - levels))),
    ])
    prod_shape = jax.ShapeDtypeStruct((pts * width // blk, blk, share * levels), BF)

    def xor_permute(x, axis, k):
        return lax.ppermute(x, axis, [(i, i ^ k) for i in range(lax.axis_size(axis))])

    def to_mate(x):
        return xor_permute(x, "pts", 1)

    def cost(shares):
        flops = 8 * slots * blk * width * share * levels * shares
        return pl.CostEstimate(flops=flops, bytes_accessed=0, transcendentals=0)

    def local(turned, wanted, prod=None, fields=()):
        args = [cols, ens, matrices] + list(fields) + ([] if prod is None else [prod])
        outs = [jax.ShapeDtypeStruct((len(some), levels, width), BF) for _, some in wanted]
        cores = (1,) if len(fields) == 1 else tuple(range(len(fields)))
        return pl.pallas_call(
            functools.partial(sums_kernel, cores, turned, wanted),
            out_shape=outs + ([prod_shape] if fields else []),
            in_specs=[ANY] + [VMEM] * (len(args) - 1),
            out_specs=[VMEM] * (len(outs) + bool(fields)),
            scratch_shapes=[pltpu.SMEM(cols.shape, jnp.int32), pltpu.SemaphoreType.DMA],
            input_output_aliases={len(args) - 1: len(outs)} if len(fields) == 1 else {},
            compiler_params=PARAMS,
            cost_estimate=cost(sum(len(some) for _, some in wanted)),
        )(*args)

    def early_products(field):
        return pl.pallas_call(
            products_kernel, out_shape=prod_shape, in_specs=[VMEM] * 2, out_specs=VMEM, compiler_params=PARAMS,
            cost_estimate=cost(1),
        )(ens, field)

    def sum_over_mem(total):
        step = 1
        while step < mem:
            rounded = total.astype(BF)
            total = rounded.astype(F32) + xor_permute(rounded, "mem", 2 * step - 1).astype(F32)
            step *= 2
        return total

    def cov_sum(turned, fields, prod=None):
        mate, prod = local(turned, [(1, far + [0])], prod=prod, fields=fields)
        got = to_mate(mate)
        (own,) = local(turned, [(0, far)], prod=prod)
        chip = (own.astype(F32) + got[:-1].astype(F32)).astype(BF)
        arrived = [xor_permute(chip[i], "pts", 2 * k) for i, k in reversed(list(enumerate(far)))]
        prod, _ = lax.optimization_barrier((prod, chip))
        (own,) = local(turned, [(0, [0])], prod=prod)
        total = own[0].astype(F32) + got[-1].astype(F32)
        for a in arrived:
            total = total + a.astype(F32)
        return sum_over_mem(total)

    rounded = increment.astype(BF)
    turned = chips == mem
    if turned:
        pairs = [(p * mem + z, (p ^ (2 * z)) * mem + z) for p in range(pts) for z in range(mem)]
        fetched = passed_on(lax.ppermute(rounded, ("pts", "mem"), pairs))
        same = jnp.stack([fetched] + [xor_permute(fetched, "mem", k) for k in range(1, mem)])
    else:
        same = jnp.stack([rounded] + [xor_permute(rounded, "pts", 2 * k) for k in range(1, chips)])

    same, matrices = lax.optimization_barrier((same, matrices))
    ens = lax.all_to_all(
        ensemble.reshape(pts, share, levels, width), "pts", split_axis=0, concat_axis=0, tiled=True
    )
    first_sum = cov_sum(turned, (same, to_mate(same)))

    rounded = (first_sum * obs_weight).astype(BF)
    same = jnp.stack([rounded] + [xor_permute(rounded, "pts", 2 * k) for k in range(1, chips)])
    prod = early_products(same)
    first_sum, prod = lax.optimization_barrier((first_sum, prod))
    weighted = first_sum * obs_weight
    applied = cov_sum(False, (to_mate(same),), prod)
    return weighted, applied


def solution(mesh):
    return jax.shard_map(
        per_device,
        mesh=mesh,
        in_specs=(P("mem", None, "pts"), P(None, "pts"), P(None, "pts"), P(), P(), P()),
        out_specs=(P(None, "pts"), P(None, "pts")),
        check_vma=False,
    )
```

```python
import functools

import jax
import jax.numpy as jnp
from jax import lax
from jax.experimental import pallas as pl
from jax.experimental.pallas import tpu as pltpu
from jax.sharding import PartitionSpec as P

BF = jnp.bfloat16
F32 = jnp.float32
VMEM = pl.BlockSpec(memory_space=pltpu.VMEM)
ANY = pl.BlockSpec(memory_space=pl.ANY)
PARAMS = pltpu.CompilerParams(vmem_limit_bytes=24 * 2**20)
COLUMNS = 4096
HOLD = 50 * 10**9


def products(me, turn, core, ens_ref, field_ref, prod_ref):
    _, members, levels, width = ens_ref.shape
    blk = prod_ref.shape[1]
    per = width // blk
    for k in range(field_ref.shape[0]):
        share = me ^ (2 * k + core)
        f = field_ref[k ^ turn]
        for m in range(members):
            product = (ens_ref[share, m] * f).T
            for j in range(per):
                prod_ref[share * per + j, :, m * levels:(m + 1) * levels] = product[j * blk:(j + 1) * blk]


def local_sums(shares, cols_ref, ens_ref, mat_ref, prod_ref, out_ref):
    _, members, levels, width = ens_ref.shape
    slots, blk = cols_ref.shape[0], prod_ref.shape[1]
    per = width // blk
    table = jnp.concatenate([mat_ref[s * blk:(s + 1) * blk, :blk] for s in range(slots)], axis=1)
    vertical = mat_ref[slots * blk:, :levels]
    batch = max(1, COLUMNS // (per * members * levels))
    for start in range(0, len(shares), batch):
        chosen = shares[start:start + batch]
        picked = []
        for share in chosen:
            for j in range(per):
                row = share * per + j
                picked.append(jnp.concatenate([prod_ref[cols_ref[s, row]] for s in range(slots)], axis=0))
        horiz = jnp.dot(table, jnp.concatenate(picked, axis=1), preferred_element_type=F32).astype(BF)
        for c, share in enumerate(chosen):
            total = None
            for m in range(members):
                parts = []
                for j in range(per):
                    at = ((c * per + j) * members + m) * levels
                    parts.append(horiz[:, at:at + levels])
                local = lax.dot_general(
                    vertical, jnp.concatenate(parts, axis=0), (((1,), (1,)), ((), ())),
                    preferred_element_type=F32,
                )
                term = ens_ref[share, m].astype(F32) * local
                total = term if total is None else total + term
            out_ref[start + c] = total.astype(BF)


def sums_kernel(cores, turned, wanted, *refs):
    refs = list(refs)
    cols_ref, copied = refs[-2:]
    copy = pltpu.make_async_copy(refs.pop(0), cols_ref, copied)
    copy.start()
    me = lax.axis_index("pts")
    ens_ref, mat_ref = refs.pop(0), refs.pop(0)
    field_refs = [refs.pop(0) for _ in cores]
    prod_ref = refs.pop(0) if len(cores) < 2 else None
    outs = [refs.pop(0) for _ in wanted]
    if cores:
        prod_ref = refs.pop(0)
        turn = lax.axis_index("mem") if turned else 0
        for core, field_ref in zip(cores, field_refs):
            products(me, turn, core, ens_ref, field_ref, prod_ref)
    copy.wait()
    for out_ref, (core, chips) in zip(outs, wanted):
        shares = [me ^ (2 * k + core) for k in chips]
        local_sums(shares, cols_ref, ens_ref, mat_ref, prod_ref, out_ref)


def products_kernel(ens_ref, field_ref, prod_ref):
    products(lax.axis_index("pts"), 0, 0, ens_ref, field_ref, prod_ref)


def copy_kernel(x_ref, out_ref):
    out_ref[...] = x_ref[...]


def passed_on(x):
    return pl.pallas_call(
        copy_kernel, out_shape=jax.ShapeDtypeStruct(x.shape, x.dtype), in_specs=[VMEM], out_specs=VMEM,
        compiler_params=PARAMS, cost_estimate=pl.CostEstimate(flops=HOLD, bytes_accessed=0, transcendentals=0),
    )(x)


def per_device(ensemble, increment, obs_weight, vertical, block_table, block_cols):
    pts, mem = lax.axis_size("pts"), lax.axis_size("mem")
    chips = pts // 2
    members, levels, width = ensemble.shape
    slots, blk, _ = block_table.shape
    share = members // pts
    cols = block_cols.T
    far = [k ^ k >> 1 for k in range(1, chips)]
    wide = max(blk, levels)
    matrices = jnp.concatenate([
        jnp.pad(block_table.reshape(slots * blk, blk), ((0, 0), (0, wide - blk))),
        jnp.pad(vertical, ((0, 0), (0, wide - levels))),
    ])
    prod_shape = jax.ShapeDtypeStruct((pts * width // blk, blk, share * levels), BF)

    def xor_permute(x, axis, k):
        return lax.ppermute(x, axis, [(i, i ^ k) for i in range(lax.axis_size(axis))])

    def to_mate(x):
        return xor_permute(x, "pts", 1)

    def cost(shares):
        flops = 8 * slots * blk * width * share * levels * shares
        return pl.CostEstimate(flops=flops, bytes_accessed=0, transcendentals=0)

    def local(turned, wanted, prod=None, fields=()):
        args = [cols, ens, matrices] + list(fields) + ([] if prod is None else [prod])
        outs = [jax.ShapeDtypeStruct((len(some), levels, width), BF) for _, some in wanted]
        cores = (1,) if len(fields) == 1 else tuple(range(len(fields)))
        return pl.pallas_call(
            functools.partial(sums_kernel, cores, turned, wanted),
            out_shape=outs + ([prod_shape] if fields else []),
            in_specs=[ANY] + [VMEM] * (len(args) - 1),
            out_specs=[VMEM] * (len(outs) + bool(fields)),
            scratch_shapes=[pltpu.SMEM(cols.shape, jnp.int32), pltpu.SemaphoreType.DMA],
            input_output_aliases={len(args) - 1: len(outs)} if len(fields) == 1 else {},
            compiler_params=PARAMS,
            cost_estimate=cost(sum(len(some) for _, some in wanted)),
        )(*args)

    def early_products(field):
        return pl.pallas_call(
            products_kernel, out_shape=prod_shape, in_specs=[VMEM] * 2, out_specs=VMEM, compiler_params=PARAMS,
            cost_estimate=cost(1),
        )(ens, field)

    def sum_over_mem(total):
        step = 1
        while step < mem:
            rounded = total.astype(BF)
            total = rounded.astype(F32) + xor_permute(rounded, "mem", 2 * step - 1).astype(F32)
            step *= 2
        return total

    def cov_sum(turned, fields, prod=None):
        mate, prod = local(turned, [(1, far + [0])], prod=prod, fields=fields)
        got = to_mate(mate)
        (own,) = local(turned, [(0, far)], prod=prod)
        chip = (own.astype(F32) + got[:-1].astype(F32)).astype(BF)
        arrived = [xor_permute(chip[i], "pts", 2 * k) for i, k in enumerate(far)]
        prod, _ = lax.optimization_barrier((prod, chip))
        (own,) = local(turned, [(0, [0])], prod=prod)
        total = own[0].astype(F32) + got[-1].astype(F32)
        for a in arrived:
            total = total + a.astype(F32)
        return sum_over_mem(total)

    rounded = increment.astype(BF)
    turned = chips == mem
    if turned:
        pairs = [(p * mem + z, (p ^ (2 * z)) * mem + z) for p in range(pts) for z in range(mem)]
        fetched = passed_on(lax.ppermute(rounded, ("pts", "mem"), pairs))
        same = jnp.stack([fetched] + [xor_permute(fetched, "mem", k) for k in range(1, mem)])
    else:
        same = jnp.stack([rounded] + [xor_permute(rounded, "pts", 2 * k) for k in range(1, chips)])

    same, matrices = lax.optimization_barrier((same, matrices))
    ens = lax.all_to_all(
        ensemble.reshape(pts, share, levels, width), "pts", split_axis=0, concat_axis=0, tiled=True
    )
    first_sum = cov_sum(turned, (same, to_mate(same)))

    rounded = (first_sum * obs_weight).astype(BF)
    same = jnp.stack([rounded] + [xor_permute(rounded, "pts", 2 * k) for k in range(1, chips)])
    prod = early_products(same)
    first_sum, prod = lax.optimization_barrier((first_sum, prod))
    weighted = first_sum * obs_weight
    applied = cov_sum(False, (to_mate(same),), prod)
    return weighted, applied


def solution(mesh):
    return jax.shard_map(
        per_device,
        mesh=mesh,
        in_specs=(P("mem", None, "pts"), P(None, "pts"), P(None, "pts"), P(), P(), P()),
        out_specs=(P(None, "pts"), P(None, "pts")),
        check_vma=False,
    )
```

```python
import functools

import jax
import jax.numpy as jnp
from jax import lax
from jax.experimental import pallas as pl
from jax.experimental.pallas import tpu as pltpu
from jax.sharding import PartitionSpec as P

BF = jnp.bfloat16
F32 = jnp.float32
VMEM = pl.BlockSpec(memory_space=pltpu.VMEM)
ANY = pl.BlockSpec(memory_space=pl.ANY)
PARAMS = pltpu.CompilerParams(vmem_limit_bytes=24 * 2**20)
COLUMNS = 4096
HOLD = 50 * 10**9


def products(me, turn, core, ens_ref, field_refs, prod_ref):
    _, members, levels, width = ens_ref.shape
    blk = prod_ref.shape[1]
    per = width // blk
    for i, field_ref in enumerate(field_refs):
        share = me ^ (2 * (i ^ turn) + core)
        for m in range(members):
            product = (ens_ref[share, m] * field_ref[...]).T
            for j in range(per):
                prod_ref[share * per + j, :, m * levels:(m + 1) * levels] = product[j * blk:(j + 1) * blk]


def local_sums(shares, cols_ref, ens_ref, mat_ref, prod_ref, out_ref):
    _, members, levels, width = ens_ref.shape
    slots, blk = cols_ref.shape[0], prod_ref.shape[1]
    per = width // blk
    table = jnp.concatenate([mat_ref[s * blk:(s + 1) * blk, :blk] for s in range(slots)], axis=1)
    vertical = mat_ref[slots * blk:, :levels]
    batch = max(1, COLUMNS // (per * members * levels))
    for start in range(0, len(shares), batch):
        chosen = shares[start:start + batch]
        picked = []
        for share in chosen:
            for j in range(per):
                row = share * per + j
                picked.append(jnp.concatenate([prod_ref[cols_ref[s, row]] for s in range(slots)], axis=0))
        horiz = jnp.dot(table, jnp.concatenate(picked, axis=1), preferred_element_type=F32).astype(BF)
        for c, share in enumerate(chosen):
            total = None
            for m in range(members):
                parts = []
                for j in range(per):
                    at = ((c * per + j) * members + m) * levels
                    parts.append(horiz[:, at:at + levels])
                local = lax.dot_general(
                    vertical, jnp.concatenate(parts, axis=0), (((1,), (1,)), ((), ())),
                    preferred_element_type=F32,
                )
                term = ens_ref[share, m].astype(F32) * local
                total = term if total is None else total + term
            out_ref[start + c] = total.astype(BF)


def sums_kernel(cores, turned, wanted, *refs):
    refs = list(refs)
    cols_ref, copied = refs[-2:]
    copy = pltpu.make_async_copy(refs.pop(0), cols_ref, copied)
    copy.start()
    me = lax.axis_index("pts")
    ens_ref, mat_ref = refs.pop(0), refs.pop(0)
    field_refs = [[refs.pop(0) for _ in range(ens_ref.shape[0] // 2)] for _ in cores]
    prod_ref = refs.pop(0) if len(cores) < 2 else None
    outs = [refs.pop(0) for _ in wanted]
    if cores:
        prod_ref = refs.pop(0)
        turn = lax.axis_index("mem") if turned else 0
        for core, some in zip(cores, field_refs):
            products(me, turn, core, ens_ref, some, prod_ref)
    copy.wait()
    for out_ref, (core, chips) in zip(outs, wanted):
        shares = [me ^ (2 * k + core) for k in chips]
        local_sums(shares, cols_ref, ens_ref, mat_ref, prod_ref, out_ref)


def products_kernel(ens_ref, *refs):
    products(lax.axis_index("pts"), 0, 0, ens_ref, list(refs[:-1]), refs[-1])


def copy_kernel(x_ref, out_ref):
    out_ref[...] = x_ref[...].astype(out_ref.dtype)


def passed_on(x):
    return pl.pallas_call(
        copy_kernel, out_shape=jax.ShapeDtypeStruct(x.shape, BF), in_specs=[VMEM], out_specs=VMEM,
        compiler_params=PARAMS, cost_estimate=pl.CostEstimate(flops=HOLD, bytes_accessed=0, transcendentals=0),
    )(x)


def per_device(ensemble, increment, obs_weight, vertical, block_table, block_cols):
    pts, mem = lax.axis_size("pts"), lax.axis_size("mem")
    chips = pts // 2
    members, levels, width = ensemble.shape
    slots, blk, _ = block_table.shape
    share = members // pts
    cols = block_cols.T
    far = [k ^ k >> 1 for k in range(1, chips)]
    wide = max(blk, levels)
    matrices = jnp.concatenate([
        jnp.pad(block_table.reshape(slots * blk, blk), ((0, 0), (0, wide - blk))),
        jnp.pad(vertical, ((0, 0), (0, wide - levels))),
    ])
    prod_shape = jax.ShapeDtypeStruct((pts * width // blk, blk, share * levels), BF)

    def xor_permute(x, axis, k):
        return lax.ppermute(x, axis, [(i, i ^ k) for i in range(lax.axis_size(axis))])

    def to_mate(x):
        return xor_permute(x, "pts", 1)

    def cost(shares):
        flops = 8 * slots * blk * width * share * levels * shares
        return pl.CostEstimate(flops=flops, bytes_accessed=0, transcendentals=0)

    def local(turned, wanted, prod=None, fields=()):
        args = [cols, ens, matrices] + list(fields) + ([] if prod is None else [prod])
        outs = [jax.ShapeDtypeStruct((len(some), levels, width), BF) for _, some in wanted]
        cores = () if not fields else (0, 1) if prod is None else (1,)
        return pl.pallas_call(
            functools.partial(sums_kernel, cores, turned, wanted),
            out_shape=outs + ([prod_shape] if fields else []),
            in_specs=[ANY] + [VMEM] * (len(args) - 1),
            out_specs=[VMEM] * (len(outs) + bool(fields)),
            scratch_shapes=[pltpu.SMEM(cols.shape, jnp.int32), pltpu.SemaphoreType.DMA],
            input_output_aliases={len(args) - 1: len(outs)} if len(cores) == 1 else {},
            compiler_params=PARAMS,
            cost_estimate=cost(sum(len(some) for _, some in wanted)),
        )(*args)

    def early_products(fields):
        return pl.pallas_call(
            products_kernel, out_shape=prod_shape, in_specs=[VMEM] * (1 + len(fields)), out_specs=VMEM,
            compiler_params=PARAMS, cost_estimate=cost(1),
        )(ens, *fields)

    def sum_over_mem(total):
        step = 1
        while step < mem:
            rounded = total.astype(BF)
            total = rounded.astype(F32) + xor_permute(rounded, "mem", 2 * step - 1).astype(F32)
            step *= 2
        return total

    def cov_sum(turned, fields, prod=None):
        mate, prod = local(turned, [(1, far + [0])], prod=prod, fields=fields)
        got = to_mate(mate)
        (own,) = local(turned, [(0, far)], prod=prod)
        chip = (own.astype(F32) + got[:-1].astype(F32)).astype(BF)
        arrived = [xor_permute(chip[i], "pts", 2 * k) for i, k in enumerate(far)]
        prod, _ = lax.optimization_barrier((prod, chip))
        (own,) = local(turned, [(0, [0])], prod=prod)
        total = own[0].astype(F32) + got[-1].astype(F32)
        for a in arrived:
            total = total + a.astype(F32)
        return sum_over_mem(total)

    rounded = increment.astype(BF)
    turned = chips == mem
    if turned:
        pairs = [(p * mem + z, (p ^ (2 * z)) * mem + z) for p in range(pts) for z in range(mem)]
        fetched = passed_on(lax.ppermute(increment, ("pts", "mem"), pairs))
        same = [fetched] + [xor_permute(fetched, "mem", k) for k in range(1, mem)]
    else:
        same = [rounded] + [xor_permute(rounded, "pts", 2 * k) for k in range(1, chips)]

    same[0], matrices = lax.optimization_barrier((same[0], matrices))
    ens = lax.all_to_all(
        ensemble.reshape(pts, share, levels, width), "pts", split_axis=0, concat_axis=0, tiled=True
    )
    first_sum = cov_sum(turned, same + [to_mate(x) for x in same])

    rounded = (first_sum * obs_weight).astype(BF)
    same = [rounded] + [xor_permute(rounded, "pts", 2 * k) for k in range(1, chips)]
    prod = early_products(same)
    first_sum, prod = lax.optimization_barrier((first_sum, prod))
    weighted = first_sum * obs_weight
    applied = cov_sum(False, [to_mate(x) for x in same], prod)
    return weighted, applied


def solution(mesh):
    return jax.shard_map(
        per_device,
        mesh=mesh,
        in_specs=(P("mem", None, "pts"), P(None, "pts"), P(None, "pts"), P(), P(), P()),
        out_specs=(P(None, "pts"), P(None, "pts")),
        check_vma=False,
    )
```

```python
import functools

import jax
import jax.numpy as jnp
from jax import lax
from jax.experimental import pallas as pl
from jax.experimental.pallas import tpu as pltpu
from jax.sharding import PartitionSpec as P

BF = jnp.bfloat16
F32 = jnp.float32
VMEM = pl.BlockSpec(memory_space=pltpu.VMEM)
ANY = pl.BlockSpec(memory_space=pl.ANY)
PARAMS = pltpu.CompilerParams(vmem_limit_bytes=24 * 2**20)
COLUMNS = 4096
HOLD = 50 * 10**9


def products(me, turn, core, ens_ref, field_refs, prod_ref):
    _, members, levels, width = ens_ref.shape
    blk = prod_ref.shape[1]
    per = width // blk
    for i, field_ref in enumerate(field_refs):
        share = me ^ (2 * (i ^ turn) + core)
        for m in range(members):
            product = (ens_ref[share, m] * field_ref[...]).T
            for j in range(per):
                prod_ref[share * per + j, :, m * levels:(m + 1) * levels] = product[j * blk:(j + 1) * blk]


def local_sums(shares, cols_ref, ens_ref, mat_ref, prod_ref, outs):
    _, members, levels, width = ens_ref.shape
    slots, blk = cols_ref.shape[0], prod_ref.shape[1]
    per = width // blk
    table = jnp.concatenate([mat_ref[s * blk:(s + 1) * blk, :blk] for s in range(slots)], axis=1)
    vertical = mat_ref[slots * blk:, :levels]
    batch = max(1, COLUMNS // (per * members * levels))
    for start in range(0, len(shares), batch):
        chosen = shares[start:start + batch]
        picked = []
        for share in chosen:
            for j in range(per):
                row = share * per + j
                picked.append(jnp.concatenate([prod_ref[cols_ref[s, row]] for s in range(slots)], axis=0))
        horiz = jnp.dot(table, jnp.concatenate(picked, axis=1), preferred_element_type=F32).astype(BF)
        for c, share in enumerate(chosen):
            total = None
            for m in range(members):
                parts = []
                for j in range(per):
                    at = ((c * per + j) * members + m) * levels
                    parts.append(horiz[:, at:at + levels])
                local = lax.dot_general(
                    vertical, jnp.concatenate(parts, axis=0), (((1,), (1,)), ((), ())),
                    preferred_element_type=F32,
                )
                term = ens_ref[share, m].astype(F32) * local
                total = term if total is None else total + term
            outs[start + c][...] = total.astype(BF)


def sums_kernel(cores, turned, wanted, *refs):
    refs = list(refs)
    cols_ref, copied = refs[-2:]
    copy = pltpu.make_async_copy(refs.pop(0), cols_ref, copied)
    copy.start()
    me = lax.axis_index("pts")
    ens_ref, mat_ref = refs.pop(0), refs.pop(0)
    field_refs = [[refs.pop(0) for _ in range(ens_ref.shape[0] // 2)] for _ in cores]
    prod_ref = refs.pop(0) if len(cores) < 2 else None
    outs = [refs.pop(0) for _ in wanted]
    if cores:
        prod_ref = refs.pop(0)
        turn = lax.axis_index("mem") if turned else 0
        for core, some in zip(cores, field_refs):
            products(me, turn, core, ens_ref, some, prod_ref)
    copy.wait()
    places = [(me ^ (2 * k + core), out_ref.at[i]) for out_ref, (core, some) in zip(outs, wanted) for i, k in enumerate(some)]
    local_sums([share for share, _ in places], cols_ref, ens_ref, mat_ref, prod_ref, [out for _, out in places])


def products_kernel(ens_ref, *refs):
    products(lax.axis_index("pts"), 0, 0, ens_ref, list(refs[:-1]), refs[-1])


def copy_kernel(x_ref, out_ref):
    out_ref[...] = x_ref[...].astype(out_ref.dtype)


def sum_kernel(*refs):
    total = refs[0][...].astype(F32)
    for x_ref in refs[1:-1]:
        total = total + x_ref[...].astype(F32)
    refs[-1][...] = total


def added(arrays):
    return pl.pallas_call(
        sum_kernel, out_shape=jax.ShapeDtypeStruct(arrays[0].shape, F32), in_specs=[VMEM] * len(arrays),
        out_specs=VMEM, compiler_params=PARAMS,
        cost_estimate=pl.CostEstimate(flops=HOLD // 10, bytes_accessed=0, transcendentals=0),
    )(*arrays)


def passed_on(x):
    return pl.pallas_call(
        copy_kernel, out_shape=jax.ShapeDtypeStruct(x.shape, BF), in_specs=[VMEM], out_specs=VMEM,
        compiler_params=PARAMS, cost_estimate=pl.CostEstimate(flops=HOLD, bytes_accessed=0, transcendentals=0),
    )(x)


def per_device(ensemble, increment, obs_weight, vertical, block_table, block_cols):
    pts, mem = lax.axis_size("pts"), lax.axis_size("mem")
    chips = pts // 2
    members, levels, width = ensemble.shape
    slots, blk, _ = block_table.shape
    share = members // pts
    cols = block_cols.T
    far = [k ^ k >> 1 for k in range(1, chips)]
    wide = max(blk, levels)
    matrices = jnp.concatenate([
        jnp.pad(block_table.reshape(slots * blk, blk), ((0, 0), (0, wide - blk))),
        jnp.pad(vertical, ((0, 0), (0, wide - levels))),
    ])
    prod_shape = jax.ShapeDtypeStruct((pts * width // blk, blk, share * levels), BF)

    def xor_permute(x, axis, k):
        return lax.ppermute(x, axis, [(i, i ^ k) for i in range(lax.axis_size(axis))])

    def to_mate(x):
        return xor_permute(x, "pts", 1)

    def cost(shares):
        flops = 8 * slots * blk * width * share * levels * shares
        return pl.CostEstimate(flops=flops, bytes_accessed=0, transcendentals=0)

    def local(turned, wanted, prod=None, fields=()):
        args = [cols, ens, matrices] + list(fields) + ([] if prod is None else [prod])
        outs = [jax.ShapeDtypeStruct((len(some), levels, width), BF) for _, some in wanted]
        cores = () if not fields else (0, 1) if prod is None else (1,)
        return pl.pallas_call(
            functools.partial(sums_kernel, cores, turned, wanted),
            out_shape=outs + ([prod_shape] if fields else []),
            in_specs=[ANY] + [VMEM] * (len(args) - 1),
            out_specs=[VMEM] * (len(outs) + bool(fields)),
            scratch_shapes=[pltpu.SMEM(cols.shape, jnp.int32), pltpu.SemaphoreType.DMA],
            input_output_aliases={len(args) - 1: len(outs)} if len(cores) == 1 else {},
            compiler_params=PARAMS,
            cost_estimate=cost(sum(len(some) for _, some in wanted)),
        )(*args)

    def early_products(fields):
        return pl.pallas_call(
            products_kernel, out_shape=prod_shape, in_specs=[VMEM] * (1 + len(fields)), out_specs=VMEM,
            compiler_params=PARAMS, cost_estimate=cost(1),
        )(ens, *fields)

    def sum_over_mem(total):
        step = 1
        while step < mem:
            rounded = total.astype(BF)
            total = rounded.astype(F32) + xor_permute(rounded, "mem", 2 * step - 1).astype(F32)
            step *= 2
        return total

    def cov_sum(turned, fields, prod=None):
        mate, prod = local(turned, [(1, far)], prod=prod, fields=fields)
        got = to_mate(mate)
        (own,) = local(turned, [(0, far)], prod=prod)
        chip = (own.astype(F32) + got.astype(F32)).astype(BF)
        arrived = [xor_permute(chip[far.index(k)], "pts", 2 * k) for k in sorted(far, reverse=True)]
        prod, _ = lax.optimization_barrier((prod, chip))
        mate, own = local(turned, [(1, [0]), (0, [0])], prod=prod)
        total = added(arrived) + (own[0].astype(F32) + to_mate(mate)[0].astype(F32))
        return sum_over_mem(total)

    rounded = increment.astype(BF)
    turned = chips == mem
    if turned:
        pairs = [(p * mem + z, (p ^ (2 * z)) * mem + z) for p in range(pts) for z in range(mem)]
        fetched = passed_on(lax.ppermute(increment, ("pts", "mem"), pairs))
        same = [fetched] + [xor_permute(fetched, "mem", k) for k in range(1, mem)]
    else:
        same = [rounded] + [xor_permute(rounded, "pts", 2 * k) for k in range(1, chips)]

    same[0], matrices = lax.optimization_barrier((same[0], matrices))
    ens = lax.all_to_all(
        ensemble.reshape(pts, share, levels, width), "pts", split_axis=0, concat_axis=0, tiled=True
    )
    first_sum = cov_sum(turned, same + [to_mate(x) for x in same])

    rounded = (first_sum * obs_weight).astype(BF)
    same = [rounded] + [xor_permute(rounded, "pts", 2 * k) for k in range(1, chips)]
    prod = early_products(same)
    first_sum, prod = lax.optimization_barrier((first_sum, prod))
    weighted = first_sum * obs_weight
    applied = cov_sum(False, [to_mate(x) for x in same], prod)
    return weighted, applied


def solution(mesh):
    return jax.shard_map(
        per_device,
        mesh=mesh,
        in_specs=(P("mem", None, "pts"), P(None, "pts"), P(None, "pts"), P(), P(), P()),
        out_specs=(P(None, "pts"), P(None, "pts")),
        check_vma=False,
    )
```
